128 devices in a mesh: blk: 32 (over y_lo, z, x), dp: 4 (over y_hi, core).
Axes of the slice: x: 4, y: 4 (y_hi: 2, y_lo: 2; y = y_hi * 2 + y_lo), z: 4, core: 2. Of those that a mesh axis runs over, the one named last changes fastest.
Arguments:
- hidden_rows: bfloat16 [4096, 4, 5376], P('blk'), may hold values from -320 to 320
- head_weight: bfloat16 [131072, 5376], P(('blk', 'dp')), may hold values from -1 to 1
- targets: int32 [4096], P('blk'), may hold values from 0 to 131071, as said below
Outputs:
- cross_entropy: float32 [4096, 4], P('blk')
- divergence: float32 [4096, 3], P('blk')
The draws below stay inside these ranges and needn't reach their ends.
Inputs may be any that keep to these rules, and one draw needn't show every extreme that they name: targets[t] = ((t // 128) * 4096 + o) mod 131072 for some o with 0 <= o < 16384.
All inputs are finite; a program needn't handle non-finite values.
Results may differ from the reference program's by a relative error of at most 0.0003.
Values may be sent and summed in bfloat16 or wider, within the bound.
No kernel may reach another device: no remote copies, remote signals or barrier semaphores. Data moves between devices by JAX's collectives and lax.ppermute only.
A program may use at most 128 MiB of HBM per device.

```python
import jax
import jax.numpy as jnp
from jax import lax

D = 5376
ROW_DEV = 128
TOKENS = 4096
SHARD = 4096
VOCAB = 131072
WINDOW = 16384


def head_row(key, row_id):
    table_key = jax.random.fold_in(key, 11)
    values = jax.random.normal(jax.random.fold_in(table_key, row_id), (D,), jnp.float32)
    return jnp.clip(values, -5.0, 5.0) * D ** (-0.5)


def draw_head_weight(key, part):
    index = jnp.arange(VOCAB, dtype=jnp.int32)
    source = index
    table = jax.vmap(lambda row_id: head_row(key, row_id))(source)
    return table.astype(jnp.bfloat16)


def draw_hidden_rows(key, part):
    own = jax.random.fold_in(key, 23)
    first_key, second_key = jax.random.split(own, 2)
    common = jnp.clip(jax.random.normal(first_key, (TOKENS, 1, D), jnp.float32), -6.0, 6.0)
    apart = jnp.clip(jax.random.normal(second_key, (TOKENS, 4, D), jnp.float32), -6.0, 6.0)
    factor = jnp.ones((TOKENS, 1, 1), jnp.float32)
    common_weight = jnp.array([0.8, 0.8, 0.8, 1.0], jnp.float32)
    apart_weight = jnp.array([0.6, 0.6, 0.6, 0.0], jnp.float32)
    mixed = 3.0 * factor * (common_weight[None, :, None] * common + apart_weight[None, :, None] * apart)
    return mixed.astype(jnp.bfloat16)


def draw_targets(key, part):
    own = jax.random.fold_in(key, 5)
    offsets = jax.random.randint(own, (TOKENS,), 0, WINDOW, jnp.int32)
    index = jnp.arange(TOKENS, dtype=jnp.int32)
    offsets = jnp.where(index == TOKENS - ROW_DEV, SHARD - 1, offsets)
    offsets = jnp.where(index == TOKENS - ROW_DEV + 1, SHARD, offsets)
    block = index // ROW_DEV
    return ((block * SHARD + offsets) % VOCAB).astype(jnp.int32)


def setup_inputs(seed: int = 0) -> dict:
    streams_of = jax.random.split(jax.random.key(seed), 4)
    hidden_rows = draw_hidden_rows(jax.random.fold_in(streams_of[3], 71), 0)
    head_weight = draw_head_weight(jax.random.fold_in(streams_of[3], 71), 0)
    targets = draw_targets(jax.random.fold_in(streams_of[3], 71), 0)
    return dict(hidden_rows=hidden_rows, head_weight=head_weight, targets=targets)


def block_losses(block, hidden_rows, head_weight, targets):
    row_block = lax.dynamic_slice_in_dim(hidden_rows, block * ROW_DEV, ROW_DEV, 0)
    wanted = lax.dynamic_slice_in_dim(targets, block * ROW_DEV, ROW_DEV, 0)
    vocab_ids = (block * SHARD + jnp.arange(WINDOW, dtype=jnp.int32)) % VOCAB
    window = jnp.take(head_weight, vocab_ids, axis=0)
    flattened = row_block.reshape(ROW_DEV * 4, D)
    logits = jnp.dot(flattened, window.T, preferred_element_type=jnp.float32)
    logits = logits.reshape(ROW_DEV, 4, WINDOW)
    peak = jnp.max(logits, axis=2)
    scaled = jnp.exp(logits - peak[:, :, None])
    total = jnp.sum(scaled, axis=2)
    lse = peak + jnp.log(total)
    spread = jnp.sum(scaled[:, 3:4, :] * (logits[:, 3:4, :] - logits), axis=2)
    position = ((wanted - block * SHARD) % VOCAB).astype(jnp.int32)
    target_logit = jnp.take_along_axis(logits, position[:, None, None] * jnp.ones((1, 4, 1), jnp.int32), axis=2)[:, :, 0]
    cross = lse - target_logit
    apart = spread[:, :3] / total[:, 3:4] - lse[:, 3:4] + lse[:, :3]
    return cross, apart


def reference(hidden_rows, head_weight, targets):
    blocks = jnp.arange(TOKENS // ROW_DEV, dtype=jnp.int32)
    cross, apart = lax.map(lambda block: block_losses(block, hidden_rows, head_weight, targets), blocks)
    return cross.reshape(TOKENS, 4), apart.reshape(TOKENS, 3)
```

```python
import functools

import jax
import jax.numpy as jnp
from jax import lax
from jax.experimental import pallas as pl
from jax.experimental.pallas import tpu as pltpu
from jax.sharding import PartitionSpec as P

EXITS = 4
LANES = 128
STEP = 1024
CHUNK = 32
LOW = -3.0e38
NS = 20


def rolled_up(value, by):
    return pltpu.roll(value, value.shape[0] - by, 0)


def final_exit(value, exit_id):
    return jnp.where(
        exit_id == 3,
        value,
        jnp.where(
            exit_id == 2,
            rolled_up(value, 1),
            jnp.where(exit_id == 1, rolled_up(value, 2), rolled_up(value, 3)),
        ),
    )


def fold_logits(logits, wanted, first, state, rows, columns):
    def fold(step, carry):
        here = pl.ds(pl.multiple_of(step * CHUNK, CHUNK), CHUNK)
        exit_id = lax.broadcasted_iota(jnp.int32, (CHUNK, LANES), 0) % EXITS
        lane = lax.broadcasted_iota(jnp.int32, (CHUNK, LANES), 1)
        offset = wanted[here, :] - first - lane
        slabs = [logits[here, pl.ds(LANES * i, LANES)] for i in range(columns // LANES)]
        old_peak = state[0, here, :]
        peak = old_peak
        for slab in slabs:
            peak = jnp.maximum(peak, slab)
        final_peak = final_exit(peak, exit_id)
        decay = jnp.exp(old_peak - peak)
        total = state[1, here, :] * decay
        spread = state[2, here, :] * final_exit(decay, exit_id)
        target = state[3, here, :]
        for i, slab in enumerate(slabs):
            final = final_exit(slab, exit_id)
            total = total + jnp.exp(slab - peak)
            spread = spread + jnp.exp(final - final_peak) * (final - slab)
            target = target + jnp.where(offset == LANES * i, slab, 0.0)
        state[0, here, :] = peak
        state[1, here, :] = total
        state[2, here, :] = spread
        state[3, here, :] = target
        return carry

    lax.fori_loop(0, rows // CHUNK, fold, 0)


def summary_kernel(pieces, distance, *refs):
    parts = refs[:pieces]
    starts, own_head, other_head, wanted, out, held, logits, state, sems = refs[pieces:]
    rows = held.shape[0]
    copies = []
    for i, part in enumerate(parts):
        start = pl.multiple_of(starts[i], 16)
        copies.append(
            pltpu.make_async_copy(part, held.at[pl.ds(start, part.shape[0])], sems.at[i])
        )
    for copy in copies:
        copy.start()
    state[0] = jnp.full((rows, LANES), LOW, jnp.float32)
    state[1:] = jnp.zeros((3, rows, LANES), jnp.float32)
    for copy in copies:
        copy.wait()
    first = 0
    for head in (own_head, other_head):
        for begin in range(0, head.shape[0], STEP):
            logits[...] = lax.dot_general(
                held[...],
                head[pl.ds(begin, STEP), :],
                (((1,), (1,)), ((), ())),
                preferred_element_type=jnp.float32,
            )
            fold_logits(logits, wanted.at[distance], first, state, rows, STEP)
            first += STEP
    exit_id = lax.broadcasted_iota(jnp.int32, (rows, LANES), 0) % EXITS
    peak = jnp.max(state[0], axis=1, keepdims=True)
    weight = jnp.exp(state[0] - peak)
    total = jnp.sum(state[1] * weight, axis=1, keepdims=True)
    spread = jnp.sum(state[2] * final_exit(weight, exit_id), axis=1, keepdims=True)
    target = jnp.sum(state[3], axis=1, keepdims=True)
    lane = lax.broadcasted_iota(jnp.int32, (rows, LANES), 1)
    packed = jnp.where(
        lane == 0,
        peak,
        jnp.where(lane == 1, total, jnp.where(lane == 2, spread, jnp.where(lane == 3, target, 0.0))),
    )
    out[...] = packed.T[:8]


def summarize(parts, starts, own_head, other_head, wanted, distance):
    rows = sum(part.shape[0] for part in parts)
    width = own_head.shape[1]
    vocab = own_head.shape[0] + other_head.shape[0]
    in_place = pl.BlockSpec(memory_space=pl.ANY)
    in_vmem = pl.BlockSpec(memory_space=pltpu.VMEM)
    return pl.pallas_call(
        functools.partial(summary_kernel, len(parts), distance),
        out_shape=jax.ShapeDtypeStruct((8, rows), jnp.float32),
        in_specs=[in_place] * len(parts)
        + [pl.BlockSpec(memory_space=pltpu.SMEM)]
        + [in_vmem] * 3,
        out_specs=in_vmem,
        scratch_shapes=[
            pltpu.VMEM((rows, width), jnp.bfloat16),
            pltpu.VMEM((rows, STEP), jnp.float32),
            pltpu.VMEM((4, rows, LANES), jnp.float32),
            pltpu.SemaphoreType.DMA((len(parts),)),
        ],
        compiler_params=pltpu.CompilerParams(vmem_limit_bytes=20 * 2**20),
        cost_estimate=pl.CostEstimate(
            flops=2 * rows * vocab * width,
            bytes_accessed=2 * (rows + vocab) * width,
            transcendentals=2 * rows * vocab,
        ),
    )(*parts, starts, own_head, other_head, wanted)


def join(first, second):
    rows = first.shape[-1]
    peak = jnp.maximum(first[..., 0, :], second[..., 0, :])
    first_weight = jnp.exp(first[..., 0, :] - peak)
    second_weight = jnp.exp(second[..., 0, :] - peak)

    def of_final(weight):
        by_token = weight.reshape(weight.shape[:-1] + (rows // EXITS, EXITS))
        return jnp.broadcast_to(by_token[..., 3:4], by_token.shape).reshape(weight.shape)

    total = first[..., 1, :] * first_weight + second[..., 1, :] * second_weight
    spread = first[..., 2, :] * of_final(first_weight) + second[..., 2, :] * of_final(second_weight)
    return jnp.stack([peak, total, spread, first[..., 3, :] + second[..., 3, :]], axis=-2)


def on_device(hidden_rows, head_weight, targets):
    blocks = lax.axis_size("blk")
    pieces = lax.axis_size("dp")
    place = lax.axis_index("blk")
    column = lax.axis_index("dp")
    half, core = column // 2, column % 2
    tokens, _, width = hidden_rows.shape
    mine = tokens // 2
    shared = NS
    direct = mine - 2 * shared
    vocab = head_weight.shape[0]

    def moved(value, by, flip=0):
        pairs = []
        for b in range(blocks):
            for d in range(pieces):
                to = b + by
                twist = 2 if (to % blocks) // 16 != b // 16 and d % 2 == 1 else 0
                pairs.append((b * pieces + d, (to % blocks) * pieces + (d ^ flip ^ twist)))
        return lax.ppermute(value, ("blk", "dp"), pairs)

    def back(value, by, flip=0):
        pairs = [
            (b * pieces + d, (b - by) % blocks * pieces + (d ^ flip))
            for b in range(blocks)
            for d in range(pieces)
        ]
        return lax.ppermute(value, ("blk", "dp"), pairs)

    def swapped(value, flip):
        pairs = [(b * pieces + d, b * pieces + (d ^ flip)) for b in range(blocks) for d in range(pieces)]
        return lax.ppermute(value, ("blk", "dp"), pairs)

    def token_rows(start, count):
        return lax.dynamic_slice_in_dim(hidden_rows, start, count, 0).reshape(count * EXITS, width)

    begin = core * mine
    own_m = token_rows(begin + half * shared, shared)
    own_d = token_rows(begin + 2 * shared, direct)
    own_o = token_rows(begin + (1 - half) * shared, shared)

    r3_m = moved(own_m, 3)
    r3_d = moved(own_d, 3)
    other_head = swapped(head_weight, 1)
    r2_m = moved(r3_m, -1)
    r3_o = swapped(r3_m, 2)
    r1_m = moved(own_m, 1)
    r2_d = moved(r3_d, -1)
    r1_o = swapped(r1_m, 2)
    r2_o = swapped(r2_m, 2)
    r1_d = moved(own_d, 1)

    one_back = lax.ppermute(targets, "blk", [(b, (b + 1) % blocks) for b in range(blocks)])
    two_back = lax.ppermute(
        jnp.stack([targets, one_back]), "blk", [(b, (b + 2) % blocks) for b in range(blocks)]
    )
    wanted = jnp.stack([targets, one_back, two_back[0], two_back[1]])
    wanted = lax.dynamic_slice_in_dim(wanted, begin, mine, 1)
    local = wanted - (place * pieces + half * 2) * vocab
    inside = (local >= 0) & (local < 2 * vocab)
    local = jnp.where(inside, (local + core * vocab) % (2 * vocab), -1)
    wanted = jnp.broadcast_to(local[:, :, None, None], (4, mine, EXITS, LANES))
    wanted = wanted.reshape(4, mine * EXITS, LANES)

    ahead = shared * EXITS

    def block(m, o, d, distance):
        wrapped = (place - distance) % blocks // 16 != place // 16
        side = jnp.where(wrapped & (core == 1), 1 - half, half)
        starts = jnp.stack([side * ahead, (1 - side) * ahead, 2 * ahead + 0 * side])
        return summarize([m, o, d], starts, head_weight, other_head, wanted, distance)

    s0 = block(own_m, own_o, own_d, 0)
    s3 = back(block(r3_m, r3_o, r3_d, 3), 3)
    s1 = back(block(r1_m, r1_o, r1_d, 1), 1)
    early = join(join(s0, s3), s1)
    early = [early] + [swapped(early, flip) for flip in (1, 2, 3)]
    s2 = block(r2_m, r2_o, r2_d, 2)
    late = [back(s2, 2, flip) for flip in (0, 1, 2, 3)]
    whole = [join(a, b) for a, b in zip(early, late)]
    mine_done = join(whole[0], whole[2])
    other_done = join(whole[1], whole[3])
    low = jnp.where(core == 0, mine_done, other_done)
    high = jnp.where(core == 0, other_done, mine_done)
    done = jnp.concatenate([low, high], axis=1)
    done = done.reshape(4, tokens, EXITS)
    peak, total, spread, target = done[0], done[1], done[2], done[3]
    log_total = peak + jnp.log(total)
    cross_entropy = log_total - target
    divergence = spread[:, :3] / total[:, 3:4] - log_total[:, 3:4] + log_total[:, :3]
    return (cross_entropy, divergence)


def solution(mesh):
    in_specs = (P("blk", None, None), P(("blk", "dp"), None), P("blk"))
    out_specs = (P("blk", None), P("blk", None))
    return jax.shard_map(
        on_device, mesh=mesh, in_specs=in_specs, out_specs=out_specs, check_vma=False
    )
```

```python
import functools

import jax
import jax.numpy as jnp
from jax import lax
from jax.experimental import pallas as pl
from jax.experimental.pallas import tpu as pltpu
from jax.sharding import PartitionSpec as P

EXITS = 4
LANES = 128
STEP = 1024
CHUNK = 32
LOW = -3.0e38
FIRST = [(16, True), (32, False)]
THIRD = [(20, True), (24, False)]


def rolled_up(value, by):
    return pltpu.roll(value, value.shape[0] - by, 0)


def final_exit(value, exit_id):
    return jnp.where(
        exit_id == 3,
        value,
        jnp.where(
            exit_id == 2,
            rolled_up(value, 1),
            jnp.where(exit_id == 1, rolled_up(value, 2), rolled_up(value, 3)),
        ),
    )


def fold_logits(logits, wanted, offset, first, state, begin, columns):
    here = pl.ds(begin, CHUNK)
    exit_id = lax.broadcasted_iota(jnp.int32, (CHUNK, LANES), 0) % EXITS
    lane = lax.broadcasted_iota(jnp.int32, (CHUNK, LANES), 1)
    ahead = wanted[pl.ds(offset + begin, CHUNK), :] - first - lane
    slabs = [logits[here, pl.ds(LANES * i, LANES)] for i in range(columns // LANES)]
    old_peak = state[0, here, :]
    peak = old_peak
    for slab in slabs:
        peak = jnp.maximum(peak, slab)
    final_peak = final_exit(peak, exit_id)
    decay = jnp.exp(old_peak - peak)
    total = state[1, here, :] * decay
    spread = state[2, here, :] * final_exit(decay, exit_id)
    target = state[3, here, :]
    for i, slab in enumerate(slabs):
        final = final_exit(slab, exit_id)
        total = total + jnp.exp(slab - peak)
        spread = spread + jnp.exp(final - final_peak) * (final - slab)
        target = target + jnp.where(ahead == LANES * i, slab, 0.0)
    state[0, here, :] = peak
    state[1, here, :] = total
    state[2, here, :] = spread
    state[3, here, :] = target


def summary_kernel(pieces, offset, blocks, *refs):
    parts = refs[:pieces]
    starts, own_head, other_head, wanted = refs[pieces : pieces + 4]
    outs = refs[pieces + 4 : pieces + 4 + blocks]
    held, tiles, logits, state, sems, tile_sems = refs[pieces + 4 + blocks :]
    rows, depth = held.shape[0], tiles.shape[2]
    tile_count = tiles.shape[0]
    copies = []
    for i, part in enumerate(parts):
        start = pl.multiple_of(starts[i], 16)
        copies.append(
            pltpu.make_async_copy(part, held.at[pl.ds(start, part.shape[0])], sems.at[i])
        )
    steps = [
        (head, begin, part)
        for head in (own_head, other_head)
        for begin in range(0, own_head.shape[0], STEP)
        for part in range(0, own_head.shape[1], depth)
    ]

    def fetch(i):
        head, begin, part = steps[i]
        slot = i % tile_count
        return pltpu.make_async_copy(
            head.at[pl.ds(begin, STEP), pl.ds(part, depth)], tiles.at[slot], tile_sems.at[slot]
        )

    fetch(0).start()
    for copy in copies:
        copy.start()
    for i in range(1, tile_count - 1):
        fetch(i).start()
    state[0] = jnp.full((rows, LANES), LOW, jnp.float32)
    state[1:] = jnp.zeros((3, rows, LANES), jnp.float32)
    for copy in copies:
        copy.wait()
    parts_deep = own_head.shape[1] // depth
    waiting, first, turn = [], 0, 0
    for i, (_, _, part) in enumerate(steps):
        fetch(i).wait()
        if i + tile_count - 1 < len(steps):
            fetch(i + tile_count - 1).start()
        product = lax.dot_general(
            held[:, pl.ds(part, depth)],
            tiles[i % tile_count],
            (((1,), (1,)), ((), ())),
            preferred_element_type=jnp.float32,
        )
        for _ in range(-(-len(waiting) // (parts_deep - part // depth))):
            waiting.pop(0)()
        if part == 0:
            logits[turn] = product
        else:
            logits[turn] += product
        if part + depth == own_head.shape[1]:
            for begin in range(0, rows, CHUNK):
                waiting.append(
                    functools.partial(
                        fold_logits, logits.at[turn], wanted, offset, first, state, begin, STEP
                    )
                )
            first += STEP
            turn = 1 - turn
    for fold in waiting:
        fold()
    exit_id = lax.broadcasted_iota(jnp.int32, (rows, LANES), 0) % EXITS
    peak = jnp.max(state[0], axis=1, keepdims=True)
    weight = jnp.exp(state[0] - peak)
    total = jnp.sum(state[1] * weight, axis=1, keepdims=True)
    spread = jnp.sum(state[2] * final_exit(weight, exit_id), axis=1, keepdims=True)
    target = jnp.sum(state[3], axis=1, keepdims=True)
    lane = lax.broadcasted_iota(jnp.int32, (rows, LANES), 1)
    packed = jnp.where(
        lane == 0,
        peak,
        jnp.where(lane == 1, total, jnp.where(lane == 2, spread, jnp.where(lane == 3, target, 0.0))),
    )
    packed = packed.T
    for i, out in enumerate(outs):
        out[...] = packed[:8, i * (rows // blocks) : (i + 1) * (rows // blocks)]


def summarize(parts, starts, own_head, other_head, wanted, offset, blocks, busy):
    rows = sum(part.shape[0] for part in parts)
    width = own_head.shape[1]
    in_place = pl.BlockSpec(memory_space=pl.ANY)
    in_vmem = pl.BlockSpec(memory_space=pltpu.VMEM)
    return pl.pallas_call(
        functools.partial(summary_kernel, len(parts), offset, blocks),
        out_shape=[jax.ShapeDtypeStruct((8, rows // blocks), jnp.float32)] * blocks,
        in_specs=[in_place] * len(parts)
        + [pl.BlockSpec(memory_space=pltpu.SMEM)]
        + [in_place] * 2
        + [in_vmem],
        out_specs=[in_vmem] * blocks,
        scratch_shapes=[
            pltpu.VMEM((rows, width), jnp.bfloat16),
            pltpu.VMEM((4, STEP, width // 3), jnp.bfloat16),
            pltpu.VMEM((2, rows, STEP), jnp.float32),
            pltpu.VMEM((4, rows, LANES), jnp.float32),
            pltpu.SemaphoreType.DMA((len(parts),)),
            pltpu.SemaphoreType.DMA((4,)),
        ],
        compiler_params=pltpu.CompilerParams(vmem_limit_bytes=44 * 2**20),
        cost_estimate=pl.CostEstimate(flops=busy, bytes_accessed=0, transcendentals=0),
    )(
        *parts,
        starts,
        pltpu.with_memory_space_constraint(own_head, pltpu.HBM),
        pltpu.with_memory_space_constraint(other_head, pltpu.HBM),
        wanted,
    )


def join(first, second):
    rows = first.shape[-1]
    peak = jnp.maximum(first[..., 0, :], second[..., 0, :])
    first_weight = jnp.exp(first[..., 0, :] - peak)
    second_weight = jnp.exp(second[..., 0, :] - peak)

    def of_final(weight):
        by_token = weight.reshape(weight.shape[:-1] + (rows // EXITS, EXITS))
        return jnp.broadcast_to(by_token[..., 3:4], by_token.shape).reshape(weight.shape)

    total = first[..., 1, :] * first_weight + second[..., 1, :] * second_weight
    spread = first[..., 2, :] * of_final(first_weight) + second[..., 2, :] * of_final(second_weight)
    return jnp.stack([peak, total, spread, first[..., 3, :] + second[..., 3, :]], axis=-2)


def relayout_kernel(count, cuts, source, origin, *refs):
    outs = refs[: len(cuts)]
    tall, flat, fetch, sems = refs[len(cuts) :]
    copy = pltpu.make_async_copy(source.at[pl.ds(origin[0], count)], tall, fetch)
    copy.start()
    copy.wait()
    flat[...] = tall[...].reshape(flat.shape)
    copies = []
    for i, out in enumerate(outs):
        start = pl.multiple_of(origin[1 + i], 16)
        copies.append(
            pltpu.make_async_copy(flat.at[pl.ds(start, out.shape[0])], out, sems.at[i])
        )
    for copy in copies:
        copy.start()
    for copy in copies:
        copy.wait()


def token_rows(source, count, origin, cuts):
    width = source.shape[2]
    in_place = pl.BlockSpec(memory_space=pl.ANY)
    return pl.pallas_call(
        functools.partial(relayout_kernel, count, cuts),
        out_shape=[pltpu.HBM((cut, width), source.dtype) for cut in cuts],
        in_specs=[in_place, pl.BlockSpec(memory_space=pltpu.SMEM)],
        out_specs=[in_place] * len(cuts),
        scratch_shapes=[
            pltpu.VMEM((count, EXITS, width), source.dtype),
            pltpu.VMEM((count * EXITS, width), source.dtype),
            pltpu.SemaphoreType.DMA,
            pltpu.SemaphoreType.DMA((len(cuts),)),
        ],
        compiler_params=pltpu.CompilerParams(vmem_limit_bytes=16 * 2**20),
    )(pltpu.with_memory_space_constraint(source, pltpu.HBM), origin)


def on_device(hidden_rows, head_weight, targets):
    blocks = lax.axis_size("blk")
    pieces = lax.axis_size("dp")
    place = lax.axis_index("blk")
    column = lax.axis_index("dp")
    half, core = column // 2, column % 2
    tokens = hidden_rows.shape[0]
    mine = tokens // 2
    vocab = head_weight.shape[0]
    ring = 4

    def cut_starts(cuts, side):
        taken = sum(count for count, shared in cuts if shared)
        starts, at = [], taken
        for count, shared in cuts:
            if shared:
                starts.append(side * (mine - count) * EXITS)
            else:
                starts.append(at * EXITS + 0 * side)
                at += count
        return starts

    def exchanged_starts(cuts, side):
        return [(1 - side) * (mine - count) * EXITS for count, shared in cuts if shared]

    def permuted(value, move):
        pairs = []
        for b in range(blocks):
            for d in range(pieces):
                to = move(b, d)
                if to is not None:
                    pairs.append((b * pieces + d, to[0] % blocks * pieces + to[1]))
        return lax.ppermute(value, ("blk", "dp"), pairs)

    def crossing(b, by, d, turning):
        wraps = (b + by) % blocks // 16 != b // 16
        return (b + by, d ^ 2 if wraps and d % 2 in turning else d)

    def around(b, by):
        return b // ring * ring + (b + by) % ring

    def to_first(b, d):
        return crossing(b, (1, 3)[d % 2], d, (1,))

    def to_second(b, d):
        return crossing(b, (1, -1)[d % 2], d, (1,))

    def to_second_turned(b, d):
        return crossing(b, (1, -1)[d % 2], d, (0,))

    def up(b, d):
        return crossing(b, ring, d, (1,)) if b % ring == (1, 3)[d % 2] else None

    def to_third(b, d):
        if d % 2 == 1:
            return around(b, 1), d
        return (around(b, -1), d) if b % ring == 1 else crossing(b, 3, d, ())

    def across(flip):
        return lambda b, d: (b, d ^ flip)

    def home(by, flip=0):
        return lambda b, d: (b - by[d % 2], d ^ flip)

    back = [
        lax.ppermute(targets, "blk", [(b, (b + by) % blocks) for b in range(blocks)])
        for by in (1, 2, 3)
    ]
    begin = core * mine
    whole_third = len(THIRD) == 1 and not THIRD[0][1]
    at = cut_starts(FIRST, half)
    lead = token_rows(
        hidden_rows, FIRST[0][0], jnp.stack([begin + at[0] // EXITS, 0 * half]), [FIRST[0][0] * EXITS]
    )
    rest, back = lax.optimization_barrier((hidden_rows, back))
    cuts = FIRST[1:] + ([] if whole_third else THIRD)
    origin = [begin, 0 * half] + at[1:]
    origin += [] if whole_third else cut_starts(THIRD, half)
    own, *sent = token_rows(
        rest, mine, jnp.stack(origin), [mine * EXITS] + [count * EXITS for count, _ in cuts]
    )
    to_send = list(lead) + list(sent[: len(FIRST) - 1])
    third_send = [own] if whole_third else list(sent[len(FIRST) - 1 :])

    first, second = [None] * len(FIRST), [None] * len(FIRST)
    first[0] = permuted(to_send[0], to_first)
    lifted = [permuted(part, up) for part in third_send]
    other_head = permuted(head_weight, across(1))
    for i in range(1, len(FIRST)):
        first[i] = permuted(to_send[i], to_first)
    first_more = [permuted(part, across(2)) for part, cut in zip(first, FIRST) if cut[1]]
    uses_lifted = place % ring == jnp.where(core == 0, 1, 3)
    third = [
        permuted(jnp.where(uses_lifted, up_part, part), to_third)
        for up_part, part in zip(lifted, third_send)
    ]
    third_more = [permuted(part, across(2)) for part, cut in zip(third, THIRD) if cut[1]]

    def positions(ids):
        local = ids - (place * pieces + half * 2) * vocab
        inside = (local >= 0) & (local < 2 * vocab)
        local = jnp.where(inside, (local + core * vocab) % (2 * vocab), -1)
        spread = jnp.broadcast_to(local[..., None, None], local.shape + (EXITS, LANES))
        return spread.reshape(-1, LANES)

    own_wanted = positions(lax.dynamic_slice_in_dim(targets, begin, mine, 0))
    wanted = jnp.stack(
        [jnp.where(core == 0, back[0], back[2]), back[1], jnp.where(core == 0, back[2], back[0])]
    )
    wanted = positions(lax.dynamic_slice_in_dim(wanted, begin, mine, 1))

    def side(distance):
        wrapped = (place - distance) % blocks // 16 != place // 16
        return jnp.where(wrapped & (core == 1), 1 - half, half)

    def block(parts, starts, ids, offset, count):
        return summarize(
            parts,
            jnp.stack(starts).astype(jnp.int32),
            head_weight,
            other_head,
            ids,
            offset * mine * EXITS,
            count,
            0,
        )

    def placed(cuts, side, at=0):
        starts = cut_starts(cuts, side) + exchanged_starts(cuts, side)
        return [start + at * mine * EXITS for start in starts]

    first_side, second_side = side(jnp.where(core == 0, 1, 3)), side(2)
    third_side = side(jnp.where(core == 0, 3, 1))

    first_more, own_0 = lax.optimization_barrier((first_more, own))
    (sum_0,) = block([own_0], [0 * half], own_wanted, 0, 1)
    first[-1], sum_0 = lax.optimization_barrier((first[-1], sum_0))
    for i, (_, shared) in enumerate(FIRST):
        second[i] = permuted(first[i], to_second if shared else to_second_turned)
    second_more = [permuted(part, across(2)) for part, cut in zip(second, FIRST) if cut[1]]
    (sum_1,) = block(first + first_more, placed(FIRST, first_side), wanted, 0, 1)
    second[-1], sum_1 = lax.optimization_barrier((second[-1], sum_1))
    sum_1 = permuted(sum_1, home((1, 3)))
    early = join(sum_0, sum_1)
    sum_2, sum_3 = block(
        second + second_more + third + third_more,
        placed(FIRST, second_side) + placed(THIRD, third_side, 1),
        wanted,
        1,
        2,
    )
    late = join(permuted(sum_2, home((2, 2))), permuted(sum_3, home((3, 1))))
    whole = join(early, late)
    whole = [whole] + [permuted(whole, across(flip)) for flip in (1, 2, 3)]
    mine_done = join(whole[0], whole[2])
    other_done = join(whole[1], whole[3])
    low = jnp.where(core == 0, mine_done, other_done)
    high = jnp.where(core == 0, other_done, mine_done)
    done = jnp.concatenate([low, high], axis=1)
    done = done.reshape(4, tokens, EXITS)
    peak, total, spread, target = done[0], done[1], done[2], done[3]
    log_total = peak + jnp.log(total)
    cross_entropy = log_total - target
    divergence = spread[:, :3] / total[:, 3:4] - log_total[:, 3:4] + log_total[:, :3]
    return (cross_entropy, divergence)


def solution(mesh):
    in_specs = (P("blk", None, None), P(("blk", "dp"), None), P("blk"))
    out_specs = (P("blk", None), P("blk", None))
    return jax.shard_map(
        on_device, mesh=mesh, in_specs=in_specs, out_specs=out_specs, check_vma=False
    )
```

```python
import functools

import jax
import jax.numpy as jnp
from jax import lax
from jax.experimental import pallas as pl
from jax.experimental.pallas import tpu as pltpu
from jax.sharding import PartitionSpec as P

EXITS = 4
LANES = 128
STEP = 1024
CHUNK = 32
LOW = -3.0e38
FIRST = [(32, False), (32, False)]
THIRD = [(32, False), (32, False)]


def rolled_up(value, by):
    return pltpu.roll(value, value.shape[0] - by, 0)


def final_exit(value, exit_id):
    return jnp.where(
        exit_id == 3,
        value,
        jnp.where(
            exit_id == 2,
            rolled_up(value, 1),
            jnp.where(exit_id == 1, rolled_up(value, 2), rolled_up(value, 3)),
        ),
    )


def fold_logits(logits, wanted, offset, first, state, begin, columns):
    here = pl.ds(begin, CHUNK)
    exit_id = lax.broadcasted_iota(jnp.int32, (CHUNK, LANES), 0) % EXITS
    lane = lax.broadcasted_iota(jnp.int32, (CHUNK, LANES), 1)
    ahead = wanted[pl.ds(offset + begin, CHUNK), :] - first - lane
    slabs = [logits[here, pl.ds(LANES * i, LANES)] for i in range(columns // LANES)]
    old_peak = state[0, here, :]
    peak = old_peak
    for slab in slabs:
        peak = jnp.maximum(peak, slab)
    final_peak = final_exit(peak, exit_id)
    decay = jnp.exp(old_peak - peak)
    total = state[1, here, :] * decay
    spread = state[2, here, :] * final_exit(decay, exit_id)
    target = state[3, here, :]
    for i, slab in enumerate(slabs):
        final = final_exit(slab, exit_id)
        total = total + jnp.exp(slab - peak)
        spread = spread + jnp.exp(final - final_peak) * (final - slab)
        target = target + jnp.where(ahead == LANES * i, slab, 0.0)
    state[0, here, :] = peak
    state[1, here, :] = total
    state[2, here, :] = spread
    state[3, here, :] = target


def summary_kernel(pieces, offset, blocks, *refs):
    parts = refs[:pieces]
    starts, own_head, other_head, wanted = refs[pieces : pieces + 4]
    outs = refs[pieces + 4 : pieces + 4 + blocks]
    held, tiles, logits, state, sems, tile_sems = refs[pieces + 4 + blocks :]
    rows, depth = held.shape[0], tiles.shape[2]
    tile_count = tiles.shape[0]
    copies = []
    for i, part in enumerate(parts):
        start = pl.multiple_of(starts[i], 16)
        copies.append(
            pltpu.make_async_copy(part, held.at[pl.ds(start, part.shape[0])], sems.at[i])
        )
    steps = [
        (head, begin, part)
        for head in (own_head, other_head)
        for begin in range(0, own_head.shape[0], STEP)
        for part in range(0, own_head.shape[1], depth)
    ]

    def fetch(i):
        head, begin, part = steps[i]
        slot = i % tile_count
        return pltpu.make_async_copy(
            head.at[pl.ds(begin, STEP), pl.ds(part, depth)], tiles.at[slot], tile_sems.at[slot]
        )

    fetch(0).start()
    for copy in copies:
        copy.start()
    for i in range(1, tile_count - 1):
        fetch(i).start()
    state[0] = jnp.full((rows, LANES), LOW, jnp.float32)
    state[1:] = jnp.zeros((3, rows, LANES), jnp.float32)
    for copy in copies:
        copy.wait()
    parts_deep = own_head.shape[1] // depth
    waiting, first, turn = [], 0, 0
    for i, (_, _, part) in enumerate(steps):
        fetch(i).wait()
        if i + tile_count - 1 < len(steps):
            fetch(i + tile_count - 1).start()
        product = lax.dot_general(
            held[:, pl.ds(part, depth)],
            tiles[i % tile_count],
            (((1,), (1,)), ((), ())),
            preferred_element_type=jnp.float32,
        )
        for _ in range(-(-len(waiting) // (parts_deep - part // depth))):
            waiting.pop(0)()
        if part == 0:
            logits[turn] = product
        else:
            logits[turn] += product
        if part + depth == own_head.shape[1]:
            for begin in range(0, rows, CHUNK):
                waiting.append(
                    functools.partial(
                        fold_logits, logits.at[turn], wanted, offset, first, state, begin, STEP
                    )
                )
            first += STEP
            turn = 1 - turn
    for fold in waiting:
        fold()
    exit_id = lax.broadcasted_iota(jnp.int32, (rows, LANES), 0) % EXITS
    peak = jnp.max(state[0], axis=1, keepdims=True)
    weight = jnp.exp(state[0] - peak)
    total = jnp.sum(state[1] * weight, axis=1, keepdims=True)
    spread = jnp.sum(state[2] * final_exit(weight, exit_id), axis=1, keepdims=True)
    target = jnp.sum(state[3], axis=1, keepdims=True)
    lane = lax.broadcasted_iota(jnp.int32, (rows, LANES), 1)
    packed = jnp.where(
        lane == 0,
        peak,
        jnp.where(lane == 1, total, jnp.where(lane == 2, spread, jnp.where(lane == 3, target, 0.0))),
    )
    packed = packed.T
    for i, out in enumerate(outs):
        out[...] = packed[:8, i * (rows // blocks) : (i + 1) * (rows // blocks)]


def summarize(parts, starts, own_head, other_head, wanted, offset, blocks, busy):
    rows = sum(part.shape[0] for part in parts)
    width = own_head.shape[1]
    in_place = pl.BlockSpec(memory_space=pl.ANY)
    in_vmem = pl.BlockSpec(memory_space=pltpu.VMEM)
    return pl.pallas_call(
        functools.partial(summary_kernel, len(parts), offset, blocks),
        out_shape=[jax.ShapeDtypeStruct((8, rows // blocks), jnp.float32)] * blocks,
        in_specs=[in_place] * len(parts)
        + [pl.BlockSpec(memory_space=pltpu.SMEM)]
        + [in_place] * 2
        + [in_vmem],
        out_specs=[in_vmem] * blocks,
        scratch_shapes=[
            pltpu.VMEM((rows, width), jnp.bfloat16),
            pltpu.VMEM((4, STEP, width // 3), jnp.bfloat16),
            pltpu.VMEM((2, rows, STEP), jnp.float32),
            pltpu.VMEM((4, rows, LANES), jnp.float32),
            pltpu.SemaphoreType.DMA((len(parts),)),
            pltpu.SemaphoreType.DMA((4,)),
        ],
        compiler_params=pltpu.CompilerParams(vmem_limit_bytes=44 * 2**20),
        cost_estimate=pl.CostEstimate(flops=busy, bytes_accessed=0, transcendentals=0),
    )(
        *parts,
        starts,
        pltpu.with_memory_space_constraint(own_head, pltpu.HBM),
        pltpu.with_memory_space_constraint(other_head, pltpu.HBM),
        wanted,
    )


def join(first, second):
    rows = first.shape[-1]
    peak = jnp.maximum(first[..., 0, :], second[..., 0, :])
    first_weight = jnp.exp(first[..., 0, :] - peak)
    second_weight = jnp.exp(second[..., 0, :] - peak)

    def of_final(weight):
        by_token = weight.reshape(weight.shape[:-1] + (rows // EXITS, EXITS))
        return jnp.broadcast_to(by_token[..., 3:4], by_token.shape).reshape(weight.shape)

    total = first[..., 1, :] * first_weight + second[..., 1, :] * second_weight
    spread = first[..., 2, :] * of_final(first_weight) + second[..., 2, :] * of_final(second_weight)
    return jnp.stack([peak, total, spread, first[..., 3, :] + second[..., 3, :]], axis=-2)


def relayout_kernel(count, cuts, source, origin, *refs):
    outs = refs[: len(cuts)]
    tall, flat, fetch, sems = refs[len(cuts) :]
    copy = pltpu.make_async_copy(source.at[pl.ds(origin[0], count)], tall, fetch)
    copy.start()
    copy.wait()
    flat[...] = tall[...].reshape(flat.shape)
    copies = []
    for i, out in enumerate(outs):
        start = pl.multiple_of(origin[1 + i], 16)
        copies.append(
            pltpu.make_async_copy(flat.at[pl.ds(start, out.shape[0])], out, sems.at[i])
        )
    for copy in copies:
        copy.start()
    for copy in copies:
        copy.wait()


def token_rows(source, count, origin, cuts):
    width = source.shape[2]
    in_place = pl.BlockSpec(memory_space=pl.ANY)
    return pl.pallas_call(
        functools.partial(relayout_kernel, count, cuts),
        out_shape=[pltpu.HBM((cut, width), source.dtype) for cut in cuts],
        in_specs=[in_place, pl.BlockSpec(memory_space=pltpu.SMEM)],
        out_specs=[in_place] * len(cuts),
        scratch_shapes=[
            pltpu.VMEM((count, EXITS, width), source.dtype),
            pltpu.VMEM((count * EXITS, width), source.dtype),
            pltpu.SemaphoreType.DMA,
            pltpu.SemaphoreType.DMA((len(cuts),)),
        ],
        compiler_params=pltpu.CompilerParams(vmem_limit_bytes=16 * 2**20),
    )(pltpu.with_memory_space_constraint(source, pltpu.HBM), origin)


def on_device(hidden_rows, head_weight, targets):
    blocks = lax.axis_size("blk")
    pieces = lax.axis_size("dp")
    place = lax.axis_index("blk")
    column = lax.axis_index("dp")
    half, core = column // 2, column % 2
    tokens = hidden_rows.shape[0]
    mine = tokens // 2
    vocab = head_weight.shape[0]
    ring = 4

    def cut_starts(cuts, side):
        taken = sum(count for count, shared in cuts if shared)
        starts, at = [], taken
        for count, shared in cuts:
            if shared:
                starts.append(side * (mine - count) * EXITS)
            else:
                starts.append(at * EXITS + 0 * side)
                at += count
        return starts

    def exchanged_starts(cuts, side):
        return [(1 - side) * (mine - count) * EXITS for count, shared in cuts if shared]

    def permuted(value, move):
        pairs = []
        for b in range(blocks):
            for d in range(pieces):
                to = move(b, d)
                if to is not None:
                    pairs.append((b * pieces + d, to[0] % blocks * pieces + to[1]))
        return lax.ppermute(value, ("blk", "dp"), pairs)

    def crossing(b, by, d, turning):
        wraps = (b + by) % blocks // 16 != b // 16
        return (b + by, d ^ 2 if wraps and d % 2 in turning else d)

    def around(b, by):
        return b // ring * ring + (b + by) % ring

    def to_first(b, d):
        return crossing(b, (1, 3)[d % 2], d, (1,))

    def to_second(b, d):
        return crossing(b, (1, -1)[d % 2], d, (1,))

    def to_second_turned(b, d):
        return crossing(b, (1, -1)[d % 2], d, (0,))

    def up(b, d):
        return crossing(b, ring, d, (1,)) if b % ring == (1, 3)[d % 2] else None

    def to_third(b, d):
        if d % 2 == 1:
            return around(b, 1), d
        return (around(b, -1), d) if b % ring == 1 else crossing(b, 3, d, ())

    def across(flip):
        return lambda b, d: (b, d ^ flip)

    def home(by, flip=0):
        return lambda b, d: (b - by[d % 2], d ^ flip)

    back = [
        lax.ppermute(targets, "blk", [(b, (b + by) % blocks) for b in range(blocks)])
        for by in (1, 2, 3)
    ]
    begin = core * mine
    whole_third = len(THIRD) == 1 and not THIRD[0][1]
    at = cut_starts(FIRST, half)
    lead = token_rows(
        hidden_rows, FIRST[0][0], jnp.stack([begin + at[0] // EXITS, 0 * half]), [FIRST[0][0] * EXITS]
    )
    rest, back = lax.optimization_barrier((hidden_rows, back))
    cuts = FIRST[1:] + ([] if whole_third else THIRD)
    origin = [begin, 0 * half] + at[1:]
    origin += [] if whole_third else cut_starts(THIRD, half)
    own, *sent = token_rows(
        rest, mine, jnp.stack(origin), [mine * EXITS] + [count * EXITS for count, _ in cuts]
    )
    to_send = list(lead) + list(sent[: len(FIRST) - 1])
    third_send = [own] if whole_third else list(sent[len(FIRST) - 1 :])

    first, second = [None] * len(FIRST), [None] * len(FIRST)
    first[0] = permuted(to_send[0], to_first)
    lifted = [permuted(part, up) for part in third_send]
    other_head = permuted(head_weight, across(1))
    for i in range(1, len(FIRST)):
        first[i] = permuted(to_send[i], to_first)
    first_more = [permuted(part, across(2)) for part, cut in zip(first, FIRST) if cut[1]]
    uses_lifted = place % ring == jnp.where(core == 0, 1, 3)
    third = [
        permuted(jnp.where(uses_lifted, up_part, part), to_third)
        for up_part, part in zip(lifted, third_send)
    ]
    third_more = [permuted(part, across(2)) for part, cut in zip(third, THIRD) if cut[1]]

    def positions(ids):
        local = ids - (place * pieces + half * 2) * vocab
        inside = (local >= 0) & (local < 2 * vocab)
        local = jnp.where(inside, (local + core * vocab) % (2 * vocab), -1)
        spread = jnp.broadcast_to(local[..., None, None], local.shape + (EXITS, LANES))
        return spread.reshape(-1, LANES)

    own_wanted = positions(lax.dynamic_slice_in_dim(targets, begin, mine, 0))
    wanted = jnp.stack(
        [jnp.where(core == 0, back[0], back[2]), back[1], jnp.where(core == 0, back[2], back[0])]
    )
    wanted = positions(lax.dynamic_slice_in_dim(wanted, begin, mine, 1))

    def side(distance):
        wrapped = (place - distance) % blocks // 16 != place // 16
        return jnp.where(wrapped & (core == 1), 1 - half, half)

    def block(parts, starts, ids, offset, count):
        return summarize(
            parts,
            jnp.stack(starts).astype(jnp.int32),
            head_weight,
            other_head,
            ids,
            offset * mine * EXITS,
            count,
            0,
        )

    def placed(cuts, side, at=0):
        starts = cut_starts(cuts, side) + exchanged_starts(cuts, side)
        return [start + at * mine * EXITS for start in starts]

    first_side, second_side = side(jnp.where(core == 0, 1, 3)), side(2)
    third_side = side(jnp.where(core == 0, 3, 1))

    first_more, own_0 = lax.optimization_barrier((first_more, own))
    (sum_0,) = block([own_0], [0 * half], own_wanted, 0, 1)
    first[-1], sum_0 = lax.optimization_barrier((first[-1], sum_0))
    for i, (_, shared) in enumerate(FIRST):
        second[i] = permuted(first[i], to_second if shared else to_second_turned)
    second_more = [permuted(part, across(2)) for part, cut in zip(second, FIRST) if cut[1]]
    (sum_1,) = block(first + first_more, placed(FIRST, first_side), wanted, 0, 1)
    second[-1], sum_1 = lax.optimization_barrier((second[-1], sum_1))
    sum_1 = permuted(sum_1, home((1, 3)))
    early = join(sum_0, sum_1)
    sum_2, sum_3 = block(
        second + second_more + third + third_more,
        placed(FIRST, second_side) + placed(THIRD, third_side, 1),
        wanted,
        1,
        2,
    )
    late = join(permuted(sum_2, home((2, 2))), permuted(sum_3, home((3, 1))))
    whole = join(early, late)
    whole = [whole] + [permuted(whole, across(flip)) for flip in (1, 2, 3)]
    mine_done = join(whole[0], whole[2])
    other_done = join(whole[1], whole[3])
    low = jnp.where(core == 0, mine_done, other_done)
    high = jnp.where(core == 0, other_done, mine_done)
    done = jnp.concatenate([low, high], axis=1)
    done = done.reshape(4, tokens, EXITS)
    peak, total, spread, target = done[0], done[1], done[2], done[3]
    log_total = peak + jnp.log(total)
    cross_entropy = log_total - target
    divergence = spread[:, :3] / total[:, 3:4] - log_total[:, 3:4] + log_total[:, :3]
    return (cross_entropy, divergence)


def solution(mesh):
    in_specs = (P("blk", None, None), P(("blk", "dp"), None), P("blk"))
    out_specs = (P("blk", None), P("blk", None))
    return jax.shard_map(
        on_device, mesh=mesh, in_specs=in_specs, out_specs=out_specs, check_vma=False
    )
```
